256 devices in a mesh: seq: 64 (over x, y, z_lo, core), chan: 4 (over z_hi).
Axes of the slice: x: 4, y: 4, z: 8 (z_hi: 4, z_lo: 2; z = z_hi * 2 + z_lo), core: 2. Of those that a mesh axis runs over, the one named last changes fastest.
Arguments:
- query_stream: bfloat16 [16384, 4096], P('seq', 'chan'), may hold values from -6 to 6
- key_stream: bfloat16 [16384, 4096], P('seq', 'chan'), may hold values from -6 to 6
- value_stream: bfloat16 [16384, 4096], P('seq', 'chan'), may hold values from -6 to 6
- filters: bfloat16 [256, 16384], P('chan', 'seq'), may hold values from -0.046875 to 0.046875
- out_weight: bfloat16 [4096, 4096], P('chan'), may hold values from -0.125 to 0.125
- cotangent: bfloat16 [16384, 4096], P('seq', 'chan'), may hold values from -6 to 6
Outputs:
- output: bfloat16 [16384, 4096], P('seq', 'chan')
- query_grad: bfloat16 [16384, 4096], P('seq', 'chan')
- key_grad: bfloat16 [16384, 4096], P('seq', 'chan')
- value_grad: bfloat16 [16384, 4096], P('seq', 'chan')
The draws below stay inside these ranges and needn't reach their ends.
All inputs are finite; a program needn't handle non-finite values.
Results may differ from the reference program's by a relative error of at most 0.015.
Values may be sent and summed in bfloat16 or wider, within the bound.
A program may use at most 64 MiB of HBM per device.

```python
import jax
import jax.numpy as jnp
from jax import lax

D = 4096
SEQ = 16384
GROUPS = 256


def spiked(values, key, source, target, parts, factor):
    def block_of(axis_at):
        return (jnp.arange(values.shape[axis_at]) // (values.shape[axis_at] // parts)).reshape((-1,) + (1,) * (values.ndim - 1 - axis_at))

    first = jax.random.permutation(key, parts)[block_of(target)]
    other_side = (block_of(target) + parts // 2) % parts
    return jnp.where((block_of(source) == first) | (block_of(source) == other_side), factor * values, values)


def shard_levels(stream_key, extent, split, least, high):
    level, own = 1.0, jax.random.fold_in(stream_key, 6)
    for position, parts in split:
        heights = jnp.exp(jax.random.uniform(jax.random.fold_in(own, position), (parts,), jnp.float32, least / len(split), high / len(split)))
        level = level * jnp.repeat(heights, extent[position] // parts).reshape([-1 if axis == position else 1 for axis in range(len(extent))])
    return level


def gaussian(key, extent, spread, limit, shards=(), held_as=jnp.bfloat16):
    gain = shard_levels(key, extent, shards, -0.22, 0.18) if shards else 1.0
    values = jax.random.normal(key, extent, jnp.float32) * spread * gain
    return jnp.minimum(jnp.maximum(values, -limit), limit).astype(held_as)


def heavy_noise(stream_key, extent, width, limit, pieces, heavy, held_as=jnp.bfloat16):
    values = width * jax.random.normal(stream_key, extent, jnp.float32)
    if pieces:
        values = values * shard_levels(stream_key, extent, pieces, -0.22, 0.18)
    return jnp.clip(spiked(values, jax.random.fold_in(stream_key, 3), *heavy), -limit, limit).astype(held_as)


def setup_inputs(seed: int = 0) -> dict:
    keys = jax.random.split(jax.random.key(seed), 7)
    query_stream = gaussian(keys[0], (SEQ, D), 1.0, 6.0, ((0, 64), (1, 4)))
    key_stream = gaussian(keys[1], (SEQ, D), 1.0, 6.0, ((0, 64), (1, 4)))
    value_stream = gaussian(keys[2], (SEQ, D), 1.0, 6.0, ((0, 64), (1, 4)))
    filters = gaussian(keys[3], (GROUPS, SEQ), SEQ ** -0.5, 0.046875, ((0, 4), (1, 64)))
    out_weight = heavy_noise(keys[4], (D, D), D ** -0.5, 0.125, ((0, 4),), (0, 1, 4, 2.0))
    cotangent = gaussian(keys[5], (SEQ, D), 1.0, 6.0, ((0, 64), (1, 4)))
    return dict(query_stream=query_stream, key_stream=key_stream, value_stream=value_stream, filters=filters, out_weight=out_weight, cotangent=cotangent)


def causal_pass(row_block, filters, conjugate):
    length = row_block.shape[0]
    group_total = filters.shape[0]
    grouped_rows = row_block.T.reshape(group_total, -1, length)

    def one_group(group_pair):
        group_rows, group_filter = group_pair
        filter_spec = jnp.fft.rfft(group_filter, 2 * length)
        if conjugate:
            filter_spec = jnp.conj(filter_spec)
        signal_spec = jnp.fft.rfft(group_rows, 2 * length, axis=-1)
        return jnp.fft.irfft(signal_spec * filter_spec[None, :], 2 * length, axis=-1)[:, :length]

    result = lax.map(one_group, (grouped_rows, filters.astype(jnp.float32)))
    return result.reshape(-1, length).T


def reference(query_stream, key_stream, value_stream, filters, out_weight, cotangent):
    mixed = (key_stream.astype(jnp.float32) * value_stream.astype(jnp.float32)).astype(jnp.bfloat16)
    conv = causal_pass(mixed.astype(jnp.float32), filters, False)
    gated = (query_stream.astype(jnp.float32) * conv).astype(jnp.bfloat16)
    output = jnp.dot(gated, out_weight, preferred_element_type=jnp.float32).astype(jnp.bfloat16)
    grad_gated = lax.dot_general(cotangent, out_weight, (((1,), (1,)), ((), ())), preferred_element_type=jnp.float32).astype(jnp.bfloat16)
    query_grad = (grad_gated.astype(jnp.float32) * conv).astype(jnp.bfloat16)
    grad_conv = (grad_gated.astype(jnp.float32) * query_stream.astype(jnp.float32)).astype(jnp.bfloat16)
    grad_mixed = causal_pass(grad_conv.astype(jnp.float32), filters, True)
    key_grad = (grad_mixed * value_stream.astype(jnp.float32)).astype(jnp.bfloat16)
    value_grad = (grad_mixed * key_stream.astype(jnp.float32)).astype(jnp.bfloat16)
    return (output, query_grad, key_grad, value_grad)
```

```python
import functools

import jax
import jax.numpy as jnp
from jax import lax
from jax.experimental import pallas as pl
from jax.experimental.pallas import tpu as pltpu
from jax.sharding import PartitionSpec as P

MESH = pl.DeviceIdType.MESH
f32, bf16 = jnp.float32, jnp.bfloat16
TOK = 256
WID = 1024
SEQ = 64
CHAN = 4
SUB = 16
PAD = 16
HALF = TOK // 2
CH = 128
NCH = WID // CH


def build_toeplitz(filt, toep):
    row = lax.broadcasted_iota(jnp.int32, (CH, CH), 0)
    col = lax.broadcasted_iota(jnp.int32, (CH, CH), 1)
    keep = col >= row

    def skew(k, half):
        line = filt[k, pl.ds(half, 1), :]
        return pltpu.roll(jnp.broadcast_to(line, (CH, CH)), 0, 1, stride=1, stride_axis=0)

    def step(k, carry):
        last_roll, last = carry
        first_roll = skew(k, 0)
        first = jnp.where(keep, first_roll, last_roll).astype(bf16)
        second_roll = skew(k, 1)
        second = jnp.where(keep, second_roll, first_roll).astype(bf16)
        toep[k, 0:CH, 0:CH] = first
        toep[k, 0:CH, CH:TOK] = second
        toep[k, CH:TOK, 0:CH] = last
        toep[k, CH:TOK, CH:TOK] = first
        return second_roll, second

    zero = jnp.zeros((CH, CH), f32)
    lax.fori_loop(0, SEQ, step, (zero, zero.astype(bf16)))


def conv_blocks(x, toep, acc, adjoint):
    unit = 4
    for group in range(4):
        blocks = SEQ - 16 * group
        rows = blocks * SUB

        def step(m, _, group=group, blocks=blocks, rows=rows):
            k = 16 * group + m * unit
            if adjoint:
                part = sum(
                    lax.dot_general(
                        x[pl.ds(k + u, blocks)].reshape(rows, TOK),
                        toep[k + u],
                        (((1,), (1,)), ((), ())),
                        preferred_element_type=f32,
                    )
                    for u in range(unit)
                )
                at = pl.ds(0, rows)
            else:
                left = jnp.concatenate(
                    [
                        x[pl.ds(PAD + 16 * group - k - u, blocks)].reshape(rows, TOK)
                        for u in range(unit)
                    ],
                    axis=1,
                )
                right = toep[pl.ds(k, unit)].reshape(unit * TOK, TOK)
                part = jnp.dot(left, right, preferred_element_type=f32)
                at = pl.ds(TOK * group, rows)
            if group == 0:

                @pl.when(m == 0)
                def _():
                    acc[at] = part

                @pl.when(m > 0)
                def _():
                    acc[at] += part

            else:
                acc[at] += part
            return 0

        lax.fori_loop(0, 16 // unit, step, 0)


def kernel(
    q_hbm, k_hbm, v_hbm, f_hbm, w_hbm, c_hbm,
    out_hbm, qg_hbm, kg_hbm, vg_hbm,
    q, k, v, cot, f_own, w, f_all, toep,
    send_a, seq_x, seq_y, conv_t, q_t, gated, acc,
    send_g, seq_g, seq_z, gm_t, gg, cots,
    p_far, p_right, p_left, p_own, from_r1, from_l1, from_r2, from_l2, sum_r, sum_l,
    o_out, o_qg, o_kg, o_vg,
    load_sem, w_sem, store_sem, a2a_send, a2a_recv, ag_send, ag_recv, rs_send, rs_recv,
):
    s, c = lax.axis_index("seq"), lax.axis_index("chan")
    right, left, far = (lax.rem(c + d, CHAN) for d in (1, 3, 2))

    loads = [
        pltpu.make_async_copy(src, dst, load_sem.at[i])
        for i, (src, dst) in enumerate(
            ((k_hbm, k), (v_hbm, v), (f_hbm, f_own), (c_hbm, cot), (q_hbm, q))
        )
    ]
    for copy in loads:
        copy.start()
    w_loads = [
        pltpu.make_async_copy(w_hbm.at[:, pl.ds(o * WID, WID)], w.at[o], w_sem.at[o])
        for o in range(CHAN)
    ]
    for copy in w_loads:
        copy.start()

    barrier = pltpu.get_barrier_semaphore()

    def greet(d, _):
        pl.semaphore_signal(barrier, inc=1, device_id=(lax.rem(s + d, SEQ), c), device_id_type=MESH)
        return 0

    lax.fori_loop(1, SEQ, greet, 0)
    for other in (right, left, far):
        pl.semaphore_signal(barrier, inc=1, device_id=(s, other), device_id_type=MESH)

    def exchange(src, dst, offset, which):
        def step(d, _):
            to = lax.rem(s + d, SEQ)
            pltpu.make_async_remote_copy(
                src_ref=src.at[to],
                dst_ref=dst.at[offset + s],
                send_sem=a2a_send.at[which],
                recv_sem=a2a_recv.at[which],
                device_id=(to, c),
                device_id_type=MESH,
            ).start()
            return 0

        lax.fori_loop(1, SEQ, step, 0)

    def received(dst, which):
        part = dst.at[pl.ds(0, SEQ - 1)]
        pltpu.make_async_copy(part, part, a2a_recv.at[which]).wait()

    def sent(src, which):
        part = src.at[pl.ds(0, SEQ - 1)]
        pltpu.make_async_copy(part, part, a2a_send.at[which]).wait()

    def chan_copy(src, dst, to, send, recv):
        return pltpu.make_async_remote_copy(
            src_ref=src,
            dst_ref=dst,
            send_sem=send,
            recv_sem=recv,
            device_id=(s, to),
            device_id_type=MESH,
        )

    loads[0].wait()
    loads[1].wait()

    def mix(j, _):
        at = pl.ds(pl.multiple_of(j * CH, CH), CH)
        mixed = (k[:, at].astype(f32) * v[:, at].astype(f32)).astype(bf16)
        turned = mixed.astype(f32).T.astype(bf16)
        send_a[pl.ds(j * (CH // SUB), CH // SUB)] = turned.reshape(CH // SUB, SUB, TOK)
        return 0

    lax.fori_loop(0, NCH, mix, 0)
    loads[2].wait()
    loads[3].wait()
    pl.semaphore_wait(barrier, SEQ + CHAN - 2)

    low, high = pl.ds(0, HALF), pl.ds(HALF, HALF)
    first_r = chan_copy(cot.at[low], cots.at[c, low], right, ag_send.at[0], ag_recv.at[0])
    first_l = chan_copy(cot.at[high], cots.at[c, high], left, ag_send.at[1], ag_recv.at[1])
    second_r = chan_copy(cot.at[high], cots.at[c, high], right, ag_send.at[2], ag_recv.at[2])
    second_l = chan_copy(cot.at[low], cots.at[c, low], left, ag_send.at[3], ag_recv.at[3])
    on_r = chan_copy(cots.at[left, low], cots.at[left, low], right, ag_send.at[4], ag_recv.at[4])
    on_l = chan_copy(cots.at[right, high], cots.at[right, high], left, ag_send.at[5], ag_recv.at[5])
    first_r.start()
    first_l.start()
    exchange(f_own, f_all, 0, 0)
    exchange(send_a, seq_x, PAD, 1)
    second_r.start()
    second_l.start()
    f_all[s] = f_own[s]
    seq_x[PAD + s] = send_a[s]
    seq_x[0:PAD] = jnp.zeros((PAD, SUB, TOK), bf16)
    seq_g[SEQ : SEQ + PAD] = jnp.zeros((PAD, SUB, TOK), bf16)

    loads[4].wait()

    def turn_q(j, _):
        at = pl.ds(pl.multiple_of(j * CH, CH), CH)
        q_t[pl.ds(pl.multiple_of(j * CH, CH), CH), :] = q[:, at].astype(f32).T.astype(bf16)
        return 0

    lax.fori_loop(0, NCH, turn_q, 0)

    received(f_all, 0)
    build_toeplitz(f_all, toep)

    first_r.wait_recv()
    on_r.start()
    first_l.wait_recv()
    on_l.start()

    received(seq_x, 1)
    conv_blocks(seq_x, toep, acc, False)

    def round_into(dst, j):
        rows = pl.ds(pl.multiple_of(j * CH, CH), CH)
        dst[pl.ds(j * (CH // SUB), CH // SUB)] = (
            acc[rows, :].astype(bf16).reshape(CH // SUB, SUB, TOK)
        )
        return 0

    lax.fori_loop(0, NCH, lambda j, _: round_into(seq_y, j), 0)
    exchange(seq_y, conv_t, 0, 2)
    conv_t[s] = seq_y[s]

    for copy in w_loads:
        copy.wait()

    def grad_part(owner, block, start):
        def step(j, _):
            rows = pl.ds(pl.multiple_of(j * TOK, TOK), TOK)
            part = lax.dot_general(
                w[owner, rows, :], block[...], (((1,), (1,)), ((), ())), preferred_element_type=f32
            )
            if start:
                gg[rows, :] = part
            else:
                gg[rows, :] += part
            return 0

        lax.fori_loop(0, WID // TOK, step, 0)

    grad_part(c, cot, True)
    second_r.wait_recv()
    grad_part(left, cots.at[left], False)
    second_l.wait_recv()
    grad_part(right, cots.at[right], False)

    received(conv_t, 2)

    def gate(j, _):
        at = pl.ds(pl.multiple_of(j * CH, CH), CH)
        conv = conv_t[pl.ds(j * (CH // SUB), CH // SUB)].reshape(CH, TOK)
        turned = (q_t[at, :].astype(f32) * conv.astype(f32)).astype(bf16)
        gated[:, at] = turned.astype(f32).T.astype(bf16)
        return 0

    lax.fori_loop(0, NCH, gate, 0)

    def output_part(owner, dst, keep=None, keep_rows=None):
        def step(j, _):
            at = pl.ds(pl.multiple_of(j * TOK, TOK), TOK)
            part = jnp.dot(gated[...], w[owner, :, at], preferred_element_type=f32)
            dst[:, at] = part.astype(dst.dtype)
            if keep is not None:
                keep[:, at] = part[keep_rows]
            return 0

        lax.fori_loop(0, WID // TOK, step, 0)

    output_part(far, p_far)
    far_r = chan_copy(p_far.at[low], from_l1, right, rs_send.at[0], rs_recv.at[0])
    far_l = chan_copy(p_far.at[high], from_r1, left, rs_send.at[1], rs_recv.at[1])
    far_r.start()
    far_l.start()
    output_part(right, p_right, sum_r, slice(0, HALF))
    near_r = chan_copy(p_right.at[high], from_l2.at[high], right, rs_send.at[2], rs_recv.at[2])
    near_r.start()
    output_part(left, p_left, sum_l, slice(HALF, TOK))
    near_l = chan_copy(p_left.at[low], from_r2.at[low], left, rs_send.at[3], rs_recv.at[3])
    near_l.start()

    on_r.wait_recv()
    on_l.wait_recv()
    grad_part(far, cots.at[far], False)

    def to_grad_conv(j, _):
        at = pl.ds(pl.multiple_of(j * CH, CH), CH)
        rounded = gg[at, :].astype(bf16).astype(f32)
        grad_conv = (rounded * q_t[at, :].astype(f32)).astype(bf16)
        send_g[pl.ds(j * (CH // SUB), CH // SUB)] = grad_conv.reshape(CH // SUB, SUB, TOK)
        return 0

    lax.fori_loop(0, NCH, to_grad_conv, 0)
    exchange(send_g, seq_g, 0, 3)
    seq_g[s] = send_g[s]

    output_part(c, p_own)

    def to_query_grad(j, _):
        at = pl.ds(pl.multiple_of(j * CH, CH), CH)
        conv = conv_t[pl.ds(j * (CH // SUB), CH // SUB)].reshape(CH, TOK)
        turned = gg[at, :].astype(bf16).astype(f32) * conv.astype(f32)
        o_qg[:, at] = turned.T.astype(bf16)
        return 0

    lax.fori_loop(0, NCH, to_query_grad, 0)
    store_qg = pltpu.make_async_copy(o_qg, qg_hbm, store_sem.at[0])
    store_qg.start()

    far_r.wait_recv()
    p_right[low, :] = (sum_r[...] + from_l1[...].astype(f32)).astype(bf16)
    pass_r = chan_copy(p_right.at[low], from_l2.at[low], right, rs_send.at[4], rs_recv.at[4])
    pass_r.start()
    far_l.wait_recv()
    p_left[high, :] = (sum_l[...] + from_r1[...].astype(f32)).astype(bf16)
    pass_l = chan_copy(p_left.at[high], from_r2.at[high], left, rs_send.at[5], rs_recv.at[5])
    pass_l.start()

    received(seq_g, 3)
    conv_blocks(seq_g, toep, acc, True)
    lax.fori_loop(0, NCH, lambda j, _: round_into(seq_z, j), 0)
    exchange(seq_z, gm_t, 0, 4)
    gm_t[s] = seq_z[s]

    near_r.wait_recv()
    near_l.wait_recv()
    pass_r.wait_recv()
    pass_l.wait_recv()

    def to_output(j, _):
        at = pl.ds(pl.multiple_of(j * CH, CH), CH)
        o_out[:, at] = (
            p_own[:, at] + from_l2[:, at].astype(f32) + from_r2[:, at].astype(f32)
        ).astype(bf16)
        return 0

    lax.fori_loop(0, NCH, to_output, 0)
    store_out = pltpu.make_async_copy(o_out, out_hbm, store_sem.at[1])
    store_out.start()

    received(gm_t, 4)

    def to_grads(j, _):
        at = pl.ds(pl.multiple_of(j * CH, CH), CH)
        grad = gm_t[pl.ds(j * (CH // SUB), CH // SUB)].reshape(CH, TOK).astype(f32).T
        o_kg[:, at] = (grad * v[:, at].astype(f32)).astype(bf16)
        o_vg[:, at] = (grad * k[:, at].astype(f32)).astype(bf16)
        return 0

    lax.fori_loop(0, NCH, to_grads, 0)
    store_kg = pltpu.make_async_copy(o_kg, kg_hbm, store_sem.at[2])
    store_vg = pltpu.make_async_copy(o_vg, vg_hbm, store_sem.at[3])
    store_kg.start()
    store_vg.start()

    sent(f_own, 0)
    for which, src in ((1, send_a), (2, seq_y), (3, send_g), (4, seq_z)):
        sent(src, which)
    for copy in (first_r, first_l, second_r, second_l, on_r, on_l):
        copy.wait_send()
    for copy in (far_r, far_l, near_r, near_l, pass_r, pass_l):
        copy.wait_send()
    for copy in (store_qg, store_out, store_kg, store_vg):
        copy.wait()


def local(query, key, value, filters, weight, cotangent):
    lines = filters.astype(f32).reshape(SEQ, 2, CH)
    stream = jax.ShapeDtypeStruct((TOK, WID), bf16)
    here = pl.BlockSpec(memory_space=pl.ANY)
    rows = pltpu.VMEM((TOK, WID), bf16)
    turned = pltpu.VMEM((SEQ, SUB, TOK), bf16)
    padded = pltpu.VMEM((SEQ + PAD, SUB, TOK), bf16)
    lines_at = pltpu.VMEM((SEQ, 2, CH), f32)
    half = pltpu.VMEM((HALF, WID), bf16)
    half_sum = pltpu.VMEM((HALF, WID), f32)
    dma = pltpu.SemaphoreType.DMA
    return pl.pallas_call(
        kernel,
        out_shape=(stream,) * 4,
        in_specs=[here] * 6,
        out_specs=(here,) * 4,
        scratch_shapes=[
            rows, rows, rows, rows,
            lines_at,
            pltpu.VMEM((CHAN, WID, WID), bf16),
            lines_at,
            pltpu.VMEM((SEQ, TOK, TOK), bf16),
            turned, padded, turned, turned,
            pltpu.VMEM((WID, TOK), bf16),
            rows,
            pltpu.VMEM((WID, TOK), f32),
            turned, padded, turned, turned,
            pltpu.VMEM((WID, TOK), f32),
            pltpu.VMEM((CHAN, TOK, WID), bf16),
            rows, rows, rows,
            pltpu.VMEM((TOK, WID), f32),
            half, half, rows, rows,
            half_sum, half_sum,
            rows, rows, rows, rows,
            dma((5,)), dma((CHAN,)), dma((4,)), dma((5,)), dma((5,)),
            dma((6,)), dma((6,)), dma((6,)), dma((6,)),
        ],
        compiler_params=pltpu.CompilerParams(
            collective_id=0, has_side_effects=True, vmem_limit_bytes=56 << 20
        ),
        cost_estimate=pl.CostEstimate(
            flops=18_000_000_000, bytes_accessed=12 << 20, transcendentals=0
        ),
    )(query, key, value, lines, weight, cotangent)


def solution(mesh):
    split = P("seq", "chan")
    return jax.shard_map(
        local,
        mesh=mesh,
        in_specs=(split, split, split, P("chan", "seq"), P("chan", None), split),
        out_specs=(split,) * 4,
        check_vma=False,
    )
```

```python
import functools

import jax
import jax.numpy as jnp
from jax import lax
from jax.experimental import pallas as pl
from jax.experimental.pallas import tpu as pltpu
from jax.sharding import PartitionSpec as P

MESH = pl.DeviceIdType.MESH
f32, bf16 = jnp.float32, jnp.bfloat16
TOK = 256
WID = 1024
SEQ = 64
CHAN = 4
SUB = 16
PAD = 16
HALF = TOK // 2
CH = 128
NCH = WID // CH
PART = 16
PARTS = SEQ // PART
ROW = CH // SUB


def build_toeplitz(filt, toep):
    row = lax.broadcasted_iota(jnp.int32, (CH, CH), 0)
    col = lax.broadcasted_iota(jnp.int32, (CH, CH), 1)
    keep = col >= row

    def skew(k, half):
        line = filt[k, pl.ds(half, 1), :]
        return pltpu.roll(jnp.broadcast_to(line, (CH, CH)), 0, 1, stride=1, stride_axis=0)

    def step(k, carry):
        last_roll, last = carry
        first_roll = skew(k, 0)
        first = jnp.where(keep, first_roll, last_roll).astype(bf16)
        second_roll = skew(k, 1)
        second = jnp.where(keep, second_roll, first_roll).astype(bf16)
        toep[k, 0:CH, 0:CH] = first
        toep[k, 0:CH, CH:TOK] = second
        toep[k, CH:TOK, 0:CH] = last
        toep[k, CH:TOK, CH:TOK] = first
        return second_roll, second

    zero = jnp.zeros((CH, CH), f32)
    lax.fori_loop(0, SEQ, step, (zero, zero.astype(bf16)))


def conv_chunk(x, toep, acc, chunk, adjoint):
    unit = 8

    def step(m, _):
        k = m * unit
        first = PART * chunk + k if adjoint else PAD + PART * chunk - k
        sign = 1 if adjoint else -1
        left = jnp.concatenate(
            [x[pl.ds(first + sign * u, PART)].reshape(PART * SUB, TOK) for u in range(unit)], axis=1
        )
        if adjoint:
            right = jnp.concatenate([toep[k + u] for u in range(unit)], axis=1)
            part = lax.dot_general(
                left, right, (((1,), (1,)), ((), ())), preferred_element_type=f32
            )
        else:
            right = toep[pl.ds(k, unit)].reshape(unit * TOK, TOK)
            part = jnp.dot(left, right, preferred_element_type=f32)
        acc[...] += part
        return 0

    acc[...] = jnp.zeros_like(acc)
    steps = PART // unit
    lax.fori_loop(0, (PARTS - chunk) * steps if adjoint else (chunk + 1) * steps, step, 0)


def kernel(
    q_hbm, k_hbm, v_hbm, f_hbm, w_hbm, c_hbm,
    gm_t, qg_hbm, own_hbm, from_r2, from_l2,
    q, k, v, cot, f_raw, f_own, w, f_all, toep,
    send_a, seq_x, seq_y, conv_t, q_t, gated, acc,
    send_g, seq_g, seq_z, gg, cots,
    p_far, p_right, p_left, p_own, from_r1, from_l1, sum_r, sum_l, o_qg,
    load_sem, w_sem, store_sem, a2a_send, a2a_recv, ag_send, ag_recv, rs_send, rs_recv,
):
    s, c = lax.axis_index("seq"), lax.axis_index("chan")
    right, left, far = (lax.rem(c + d, CHAN) for d in (1, 3, 2))

    loads = [
        pltpu.make_async_copy(src, dst, load_sem.at[i])
        for i, (src, dst) in enumerate(
            ((k_hbm, k), (v_hbm, v), (f_hbm, f_raw), (c_hbm, cot), (q_hbm, q))
        )
    ]
    for copy in loads:
        copy.start()
    w_loads = [
        pltpu.make_async_copy(w_hbm.at[:, pl.ds(o * WID, WID)], w.at[o], w_sem.at[o])
        for o in range(CHAN)
    ]
    for copy in w_loads:
        copy.start()

    barrier = pltpu.get_barrier_semaphore()

    def greet(d, _):
        pl.semaphore_signal(barrier, inc=1, device_id=(lax.rem(s + d, SEQ), c), device_id_type=MESH)
        return 0

    lax.fori_loop(1, SEQ, greet, 0)
    for other in (right, left, far):
        pl.semaphore_signal(barrier, inc=1, device_id=(s, other), device_id_type=MESH)

    def send_block(src, dst, offset, which, to):
        @pl.when(to != s)
        def _():
            pltpu.make_async_remote_copy(
                src_ref=src.at[to],
                dst_ref=dst.at[offset + s],
                send_sem=a2a_send.at[which],
                recv_sem=a2a_recv.at[which],
                device_id=(to, c),
                device_id_type=MESH,
            ).start()

    def send_blocks(src, dst, offset, which, first, count):
        def step(d, _):
            send_block(src, dst, offset, which, first + lax.rem(lax.rem(s, count) + d, count))
            return 0

        lax.fori_loop(0, count, step, 0)

    def convolve(x, out, dst, which, adjoint):
        def step(i, _):
            chunk = lax.rem(s // PART + i, PARTS)
            conv_chunk(x, toep, acc, chunk, adjoint)
            at = pl.multiple_of(chunk * PART, PART)
            out[pl.ds(at, PART)] = acc[...].astype(bf16).reshape(PART, SUB, TOK)
            send_blocks(out, dst, 0, which, chunk * PART, PART)
            return 0

        lax.fori_loop(0, PARTS, step, 0)

    def received(dst, which):
        part = dst.at[pl.ds(0, SEQ - 1)]
        pltpu.make_async_copy(part, part, a2a_recv.at[which]).wait()

    def sent(src, which):
        part = src.at[pl.ds(0, SEQ - 1)]
        pltpu.make_async_copy(part, part, a2a_send.at[which]).wait()

    def chan_copy(src, dst, to, send, recv):
        return pltpu.make_async_remote_copy(
            src_ref=src,
            dst_ref=dst,
            send_sem=send,
            recv_sem=recv,
            device_id=(s, to),
            device_id_type=MESH,
        )

    pl.semaphore_wait(barrier, SEQ + CHAN - 2)

    low, high = pl.ds(0, HALF), pl.ds(HALF, HALF)
    first_r = chan_copy(c_hbm.at[low], cots.at[c, low], right, ag_send.at[0], ag_recv.at[0])
    first_l = chan_copy(c_hbm.at[high], cots.at[c, high], left, ag_send.at[1], ag_recv.at[1])
    second_r = chan_copy(c_hbm.at[high], cots.at[c, high], right, ag_send.at[2], ag_recv.at[2])
    second_l = chan_copy(c_hbm.at[low], cots.at[c, low], left, ag_send.at[3], ag_recv.at[3])
    on_r = chan_copy(cots.at[left, low], cots.at[left, low], right, ag_send.at[4], ag_recv.at[4])
    on_l = chan_copy(cots.at[right, high], cots.at[right, high], left, ag_send.at[5], ag_recv.at[5])
    first_r.start()
    first_l.start()

    loads[2].wait()
    lines = f_raw[...].astype(f32)
    f_own[:, 0, :] = lines[:, 0:CH]
    f_own[:, 1, :] = lines[:, CH:TOK]
    send_blocks(f_own, f_all, 0, 0, 0, SEQ)
    loads[0].wait()
    loads[1].wait()

    def mix(i, _):
        j = lax.rem(s // ROW + i, NCH)
        at = pl.ds(pl.multiple_of(j * CH, CH), CH)
        mixed = (k[:, at].astype(f32) * v[:, at].astype(f32)).astype(bf16)
        turned = mixed.astype(f32).T.astype(bf16)
        send_a[pl.ds(j * ROW, ROW)] = turned.reshape(ROW, SUB, TOK)
        send_blocks(send_a, seq_x, PAD, 1, j * ROW, ROW)
        return 0

    lax.fori_loop(0, NCH, mix, 0)
    second_r.start()
    second_l.start()
    f_all[s] = f_own[s]
    seq_x[PAD + s] = send_a[s]
    seq_x[0:PAD] = jnp.zeros((PAD, SUB, TOK), bf16)
    seq_g[SEQ : SEQ + PAD] = jnp.zeros((PAD, SUB, TOK), bf16)

    loads[4].wait()

    def turn_q(j, _):
        at = pl.ds(pl.multiple_of(j * CH, CH), CH)
        q_t[pl.ds(pl.multiple_of(j * CH, CH), CH), :] = q[:, at].astype(f32).T.astype(bf16)
        return 0

    lax.fori_loop(0, NCH, turn_q, 0)

    received(f_all, 0)
    build_toeplitz(f_all, toep)

    first_r.wait_recv()
    on_r.start()
    first_l.wait_recv()
    on_l.start()

    received(seq_x, 1)
    convolve(seq_x, seq_y, conv_t, 2, False)
    conv_t[s] = seq_y[s]

    loads[3].wait()
    for copy in w_loads:
        copy.wait()

    def grad_part(owner, block, start):
        def step(j, _):
            rows = pl.ds(pl.multiple_of(j * TOK, TOK), TOK)
            part = lax.dot_general(
                w[owner, rows, :], block[...], (((1,), (1,)), ((), ())), preferred_element_type=f32
            )
            if start:
                gg[rows, :] = part
            else:
                gg[rows, :] += part
            return 0

        lax.fori_loop(0, WID // TOK, step, 0)

    grad_part(c, cot, True)
    second_r.wait_recv()
    grad_part(left, cots.at[left], False)
    second_l.wait_recv()
    grad_part(right, cots.at[right], False)
    on_r.wait_recv()
    on_l.wait_recv()
    grad_part(far, cots.at[far], False)

    def to_grad_conv(i, _):
        j = lax.rem(s // ROW + i, NCH)
        at = pl.ds(pl.multiple_of(j * CH, CH), CH)
        rounded = gg[at, :].astype(bf16).astype(f32)
        grad_conv = (rounded * q_t[at, :].astype(f32)).astype(bf16)
        send_g[pl.ds(j * ROW, ROW)] = grad_conv.reshape(ROW, SUB, TOK)
        send_blocks(send_g, seq_g, 0, 3, j * ROW, ROW)
        return 0

    lax.fori_loop(0, NCH, to_grad_conv, 0)
    seq_g[s] = send_g[s]


    received(conv_t, 2)

    def gate(j, _):
        at = pl.ds(pl.multiple_of(j * CH, CH), CH)
        conv = conv_t[pl.ds(j * ROW, ROW)].reshape(CH, TOK)
        turned = (q_t[at, :].astype(f32) * conv.astype(f32)).astype(bf16)
        gated[:, at] = turned.astype(f32).T.astype(bf16)
        return 0

    lax.fori_loop(0, NCH, gate, 0)

    def output_part(owner, dst, keep=None, keep_rows=None):
        def step(j, _):
            at = pl.ds(pl.multiple_of(j * TOK, TOK), TOK)
            part = jnp.dot(gated[...], w[owner, :, at], preferred_element_type=f32)
            dst[:, at] = part.astype(dst.dtype)
            if keep is not None:
                keep[:, at] = part[keep_rows]
            return 0

        lax.fori_loop(0, WID // TOK, step, 0)

    far_r = chan_copy(p_far.at[low], from_l1, right, rs_send.at[0], rs_recv.at[0])
    far_l = chan_copy(p_far.at[high], from_r1, left, rs_send.at[1], rs_recv.at[1])
    near_r = chan_copy(p_right.at[high], from_l2.at[high], right, rs_send.at[2], rs_recv.at[2])
    near_l = chan_copy(p_left.at[low], from_r2.at[low], left, rs_send.at[3], rs_recv.at[3])

    output_part(far, p_far)
    far_r.start()
    far_l.start()
    output_part(right, p_right, sum_r, slice(0, HALF))
    near_r.start()
    output_part(left, p_left, sum_l, slice(HALF, TOK))
    near_l.start()
    output_part(c, p_own)
    store_own = pltpu.make_async_copy(p_own, own_hbm, store_sem.at[1])
    store_own.start()

    def to_query_grad(j, _):
        at = pl.ds(pl.multiple_of(j * CH, CH), CH)
        conv = conv_t[pl.ds(j * ROW, ROW)].reshape(CH, TOK)
        turned = gg[at, :].astype(bf16).astype(f32) * conv.astype(f32)
        o_qg[:, at] = turned.T.astype(bf16)
        return 0

    lax.fori_loop(0, NCH, to_query_grad, 0)
    store_qg = pltpu.make_async_copy(o_qg, qg_hbm, store_sem.at[0])
    store_qg.start()

    received(seq_g, 3)
    convolve(seq_g, seq_z, gm_t, 4, True)
    far_r.wait_recv()
    p_right[low, :] = (sum_r[...] + from_l1[...].astype(f32)).astype(bf16)
    pass_r = chan_copy(p_right.at[low], from_l2.at[low], right, rs_send.at[4], rs_recv.at[4])
    pass_r.start()
    far_l.wait_recv()
    p_left[high, :] = (sum_l[...] + from_r1[...].astype(f32)).astype(bf16)
    pass_l = chan_copy(p_left.at[high], from_r2.at[high], left, rs_send.at[5], rs_recv.at[5])
    pass_l.start()

    own_z = pltpu.make_async_copy(seq_z.at[s], gm_t.at[s], store_sem.at[2])
    own_z.start()

    near_r.wait_recv()
    near_l.wait_recv()
    pass_r.wait_recv()
    pass_l.wait_recv()

    received(gm_t, 4)
    own_z.wait()
    sent(f_own, 0)
    for which, src in ((1, send_a), (2, seq_y), (3, send_g), (4, seq_z)):
        sent(src, which)
    for copy in (first_r, first_l, second_r, second_l, on_r, on_l):
        copy.wait_send()
    for copy in (far_r, far_l, near_r, near_l, pass_r, pass_l):
        copy.wait_send()
    for copy in (store_qg, store_own):
        copy.wait()


def finish_kernel(gm_t, k, v, qg_in, own, from_r, from_l, out, qg, kg, vg):
    width = out.shape[1]
    grad = gm_t[...].reshape(width, TOK).astype(f32).T
    kg[...] = (grad * v[...].astype(f32)).astype(bf16)
    vg[...] = (grad * k[...].astype(f32)).astype(bf16)
    qg[...] = qg_in[...]
    total = own[...].astype(f32) + from_r[...].astype(f32) + from_l[...].astype(f32)
    out[...] = total.astype(bf16)


def local(query, key, value, filters, weight, cotangent):
    stream = jax.ShapeDtypeStruct((TOK, WID), bf16)
    here = pl.BlockSpec(memory_space=pl.ANY)
    rows = pltpu.VMEM((TOK, WID), bf16)
    turned = pltpu.VMEM((SEQ, SUB, TOK), bf16)
    padded = pltpu.VMEM((SEQ + PAD, SUB, TOK), bf16)
    lines_at = pltpu.VMEM((SEQ, 2, CH), f32)
    half = pltpu.VMEM((HALF, WID), bf16)
    half_sum = pltpu.VMEM((HALF, WID), f32)
    dma = pltpu.SemaphoreType.DMA
    gm_t, query_grad, own, from_r, from_l = pl.pallas_call(
        kernel,
        out_shape=(jax.ShapeDtypeStruct((SEQ, SUB, TOK), bf16),) + (stream,) * 4,
        in_specs=[here] * 6,
        out_specs=(here,) * 5,
        scratch_shapes=[
            rows, rows, rows, rows,
            pltpu.VMEM((SEQ, TOK), bf16),
            lines_at,
            pltpu.VMEM((CHAN, WID, WID), bf16),
            lines_at,
            pltpu.VMEM((SEQ, TOK, TOK), bf16),
            turned, padded, turned, turned,
            pltpu.VMEM((WID, TOK), bf16),
            rows,
            pltpu.VMEM((PART * SUB, TOK), f32),
            turned, padded, turned,
            pltpu.VMEM((WID, TOK), f32),
            pltpu.VMEM((CHAN, TOK, WID), bf16),
            rows, rows, rows, rows,
            half, half,
            half_sum, half_sum,
            rows,
            dma((5,)), dma((CHAN,)), dma((3,)), dma((5,)), dma((5,)),
            dma((6,)), dma((6,)), dma((6,)), dma((6,)),
        ],
        compiler_params=pltpu.CompilerParams(
            collective_id=0, has_side_effects=True, vmem_limit_bytes=56 << 20
        ),
        cost_estimate=pl.CostEstimate(
            flops=18_000_000_000, bytes_accessed=12 << 20, transcendentals=0
        ),
    )(query, key, value, filters, weight, cotangent)
    width = 256
    cols = pl.BlockSpec((TOK, width), lambda j: (0, j))
    return pl.pallas_call(
        finish_kernel,
        out_shape=(stream,) * 4,
        grid=(WID // width,),
        in_specs=[pl.BlockSpec((width // SUB, SUB, TOK), lambda j: (j, 0, 0))] + [cols] * 6,
        out_specs=(cols,) * 4,
        cost_estimate=pl.CostEstimate(
            flops=4_000_000, bytes_accessed=6 << 20, transcendentals=0
        ),
    )(gm_t, key, value, query_grad, own, from_r, from_l)


def solution(mesh):
    split = P("seq", "chan")
    return jax.shard_map(
        local,
        mesh=mesh,
        in_specs=(split, split, split, P("chan", "seq"), P("chan", None), split),
        out_specs=(split,) * 4,
        check_vma=False,
    )
```

```python
import functools

import jax
import jax.numpy as jnp
from jax import lax
from jax.experimental import pallas as pl
from jax.experimental.pallas import tpu as pltpu
from jax.sharding import PartitionSpec as P

MESH = pl.DeviceIdType.MESH
f32, bf16 = jnp.float32, jnp.bfloat16
TOK = 256
WID = 1024
SEQ = 64
CHAN = 4
SUB = 16
PAD = 16
HALF = TOK // 2
CH = 128
NCH = WID // CH
PART = 16
PARTS = SEQ // PART
ROW = CH // SUB


def build_toeplitz(filt, toep):
    row = lax.broadcasted_iota(jnp.int32, (CH, CH), 0)
    col = lax.broadcasted_iota(jnp.int32, (CH, CH), 1)
    keep = col >= row

    def skew(k, half):
        line = filt[k, pl.ds(half, 1), :]
        return pltpu.roll(jnp.broadcast_to(line, (CH, CH)), 0, 1, stride=1, stride_axis=0)

    def step(k, carry):
        last_roll, last = carry
        first_roll = skew(k, 0)
        first = jnp.where(keep, first_roll, last_roll).astype(bf16)
        second_roll = skew(k, 1)
        second = jnp.where(keep, second_roll, first_roll).astype(bf16)
        toep[k, 0:CH, 0:CH] = first
        toep[k, 0:CH, CH:TOK] = second
        toep[k, CH:TOK, 0:CH] = last
        toep[k, CH:TOK, CH:TOK] = first
        return second_roll, second

    zero = jnp.zeros((CH, CH), f32)
    lax.fori_loop(0, SEQ, step, (zero, zero.astype(bf16)), unroll=4)


def conv_chunk(x, toep, acc, chunk, adjoint):
    unit = 8

    def step(m, _):
        k = m * unit
        first = PART * chunk + k if adjoint else PAD + PART * chunk - k
        sign = 1 if adjoint else -1
        left = jnp.concatenate(
            [x[pl.ds(first + sign * u, PART)].reshape(PART * SUB, TOK) for u in range(unit)], axis=1
        )
        if adjoint:
            right = jnp.concatenate([toep[k + u] for u in range(unit)], axis=1)
            part = lax.dot_general(
                left, right, (((1,), (1,)), ((), ())), preferred_element_type=f32
            )
        else:
            right = toep[pl.ds(k, unit)].reshape(unit * TOK, TOK)
            part = jnp.dot(left, right, preferred_element_type=f32)
        acc[...] += part
        return 0

    acc[...] = jnp.zeros_like(acc)
    steps = PART // unit
    lax.fori_loop(0, (PARTS - chunk) * steps if adjoint else (chunk + 1) * steps, step, 0)


def kernel(
    q_hbm, k_hbm, v_hbm, f_hbm, w_hbm, c_hbm,
    gm_t, qg_hbm, own_hbm, from_r2, from_l2,
    q, k, v, cot, f_raw, f_own, w, f_all, toep,
    send_a, seq_x, seq_y, conv_t, q_t, gated, acc,
    send_g, seq_g, seq_z, gg, cots,
    p_far, p_right, p_left, p_own, from_r1, from_l1, sum_r, sum_l, o_qg,
    load_sem, w_sem, store_sem, a2a_send, a2a_recv, ag_send, ag_recv, rs_send, rs_recv,
):
    s, c = lax.axis_index("seq"), lax.axis_index("chan")
    right, left, far = (lax.rem(c + d, CHAN) for d in (1, 3, 2))

    loads = [
        pltpu.make_async_copy(src, dst, load_sem.at[i])
        for i, (src, dst) in enumerate(
            ((k_hbm, k), (v_hbm, v), (f_hbm, f_raw), (c_hbm, cot), (q_hbm, q))
        )
    ]
    for copy in loads:
        copy.start()
    w_loads = [
        pltpu.make_async_copy(w_hbm.at[:, pl.ds(o * WID, WID)], w.at[o], w_sem.at[o])
        for o in range(CHAN)
    ]
    for copy in w_loads:
        copy.start()

    barrier = pltpu.get_barrier_semaphore()

    def greet(d, _):
        pl.semaphore_signal(barrier, inc=1, device_id=(lax.rem(s + d, SEQ), c), device_id_type=MESH)
        return 0

    lax.fori_loop(1, SEQ, greet, 0)
    for other in (right, left, far):
        pl.semaphore_signal(barrier, inc=1, device_id=(s, other), device_id_type=MESH)

    def send_block(src, dst, offset, which, to):
        @pl.when(to != s)
        def _():
            pltpu.make_async_remote_copy(
                src_ref=src.at[to],
                dst_ref=dst.at[offset + s],
                send_sem=a2a_send.at[which],
                recv_sem=a2a_recv.at[which],
                device_id=(to, c),
                device_id_type=MESH,
            ).start()

    def send_blocks(src, dst, offset, which, first, count):
        def step(d, _):
            send_block(src, dst, offset, which, first + lax.rem(lax.rem(s, count) + d, count))
            return 0

        lax.fori_loop(0, count, step, 0)

    def convolve(x, out, dst, which, adjoint):
        def step(i, _):
            chunk = lax.rem(s // PART + i, PARTS)
            conv_chunk(x, toep, acc, chunk, adjoint)
            at = pl.multiple_of(chunk * PART, PART)
            out[pl.ds(at, PART)] = acc[...].astype(bf16).reshape(PART, SUB, TOK)
            send_blocks(out, dst, 0, which, chunk * PART, PART)
            return 0

        lax.fori_loop(0, PARTS, step, 0)

    def received(dst, which):
        part = dst.at[pl.ds(0, SEQ - 1)]
        pltpu.make_async_copy(part, part, a2a_recv.at[which]).wait()

    def sent(src, which):
        part = src.at[pl.ds(0, SEQ - 1)]
        pltpu.make_async_copy(part, part, a2a_send.at[which]).wait()

    def chan_copy(src, dst, to, send, recv):
        return pltpu.make_async_remote_copy(
            src_ref=src,
            dst_ref=dst,
            send_sem=send,
            recv_sem=recv,
            device_id=(s, to),
            device_id_type=MESH,
        )

    pl.semaphore_wait(barrier, SEQ + CHAN - 2)

    low, high = pl.ds(0, HALF), pl.ds(HALF, HALF)
    first_r = chan_copy(c_hbm.at[low], cots.at[c, low], right, ag_send.at[0], ag_recv.at[0])
    first_l = chan_copy(c_hbm.at[high], cots.at[c, high], left, ag_send.at[1], ag_recv.at[1])
    second_r = chan_copy(c_hbm.at[high], cots.at[c, high], right, ag_send.at[2], ag_recv.at[2])
    second_l = chan_copy(c_hbm.at[low], cots.at[c, low], left, ag_send.at[3], ag_recv.at[3])
    on_r = chan_copy(cots.at[left, low], cots.at[left, low], right, ag_send.at[4], ag_recv.at[4])
    on_l = chan_copy(cots.at[right, high], cots.at[right, high], left, ag_send.at[5], ag_recv.at[5])
    first_r.start()
    first_l.start()

    loads[2].wait()
    lines = f_raw[...].astype(f32)
    f_own[:, 0, :] = lines[:, 0:CH]
    f_own[:, 1, :] = lines[:, CH:TOK]
    send_blocks(f_own, f_all, 0, 0, 0, SEQ)
    loads[0].wait()
    loads[1].wait()

    def mix(i, _):
        j = lax.rem(s // ROW + i, NCH)
        at = pl.ds(pl.multiple_of(j * CH, CH), CH)
        mixed = (k[:, at].astype(f32) * v[:, at].astype(f32)).astype(bf16)
        turned = mixed.astype(f32).T.astype(bf16)
        send_a[pl.ds(j * ROW, ROW)] = turned.reshape(ROW, SUB, TOK)
        send_blocks(send_a, seq_x, PAD, 1, j * ROW, ROW)
        return 0

    lax.fori_loop(0, NCH, mix, 0, unroll=2)
    second_r.start()
    second_l.start()
    f_all[s] = f_own[s]
    seq_x[PAD + s] = send_a[s]
    seq_x[0:PAD] = jnp.zeros((PAD, SUB, TOK), bf16)
    seq_g[SEQ : SEQ + PAD] = jnp.zeros((PAD, SUB, TOK), bf16)

    loads[4].wait()

    def turn_q(j, _):
        at = pl.ds(pl.multiple_of(j * CH, CH), CH)
        q_t[pl.ds(pl.multiple_of(j * CH, CH), CH), :] = q[:, at].astype(f32).T.astype(bf16)
        return 0

    lax.fori_loop(0, NCH, turn_q, 0, unroll=2)

    received(f_all, 0)
    build_toeplitz(f_all, toep)

    first_r.wait_recv()
    on_r.start()
    first_l.wait_recv()
    on_l.start()

    received(seq_x, 1)
    convolve(seq_x, seq_y, conv_t, 2, False)
    conv_t[s] = seq_y[s]

    loads[3].wait()
    for copy in w_loads:
        copy.wait()

    def grad_part(owner, block, start):
        def step(j, _):
            rows = pl.ds(pl.multiple_of(j * TOK, TOK), TOK)
            part = lax.dot_general(
                w[owner, rows, :], block[...], (((1,), (1,)), ((), ())), preferred_element_type=f32
            )
            if start:
                gg[rows, :] = part
            else:
                gg[rows, :] += part
            return 0

        lax.fori_loop(0, WID // TOK, step, 0, unroll=2)

    grad_part(c, cot, True)
    second_r.wait_recv()
    grad_part(left, cots.at[left], False)
    second_l.wait_recv()
    grad_part(right, cots.at[right], False)
    on_r.wait_recv()
    on_l.wait_recv()
    grad_part(far, cots.at[far], False)

    def to_grad_conv(i, _):
        j = lax.rem(s // ROW + i, NCH)
        at = pl.ds(pl.multiple_of(j * CH, CH), CH)
        rounded = gg[at, :].astype(bf16).astype(f32)
        grad_conv = (rounded * q_t[at, :].astype(f32)).astype(bf16)
        send_g[pl.ds(j * ROW, ROW)] = grad_conv.reshape(ROW, SUB, TOK)
        send_blocks(send_g, seq_g, 0, 3, j * ROW, ROW)
        return 0

    lax.fori_loop(0, NCH, to_grad_conv, 0, unroll=2)
    seq_g[s] = send_g[s]


    received(conv_t, 2)

    def gate(j, _):
        at = pl.ds(pl.multiple_of(j * CH, CH), CH)
        conv = conv_t[pl.ds(j * ROW, ROW)].reshape(CH, TOK)
        turned = (q_t[at, :].astype(f32) * conv.astype(f32)).astype(bf16)
        gated[:, at] = turned.astype(f32).T.astype(bf16)
        return 0

    lax.fori_loop(0, NCH, gate, 0, unroll=2)

    def output_part(owner, dst, keep=None, keep_rows=None):
        def step(j, _):
            at = pl.ds(pl.multiple_of(j * TOK, TOK), TOK)
            part = jnp.dot(gated[...], w[owner, :, at], preferred_element_type=f32)
            dst[:, at] = part.astype(dst.dtype)
            if keep is not None:
                keep[:, at] = part[keep_rows]
            return 0

        lax.fori_loop(0, WID // TOK, step, 0, unroll=2)

    far_r = chan_copy(p_far.at[low], from_l1, right, rs_send.at[0], rs_recv.at[0])
    far_l = chan_copy(p_far.at[high], from_r1, left, rs_send.at[1], rs_recv.at[1])
    near_r = chan_copy(p_right.at[high], from_l2.at[high], right, rs_send.at[2], rs_recv.at[2])
    near_l = chan_copy(p_left.at[low], from_r2.at[low], left, rs_send.at[3], rs_recv.at[3])

    output_part(far, p_far)
    far_r.start()
    far_l.start()
    output_part(right, p_right, sum_r, slice(0, HALF))
    near_r.start()
    output_part(left, p_left, sum_l, slice(HALF, TOK))
    near_l.start()
    output_part(c, p_own)
    store_own = pltpu.make_async_copy(p_own, own_hbm, store_sem.at[1])
    store_own.start()

    def to_query_grad(j, _):
        at = pl.ds(pl.multiple_of(j * CH, CH), CH)
        conv = conv_t[pl.ds(j * ROW, ROW)].reshape(CH, TOK)
        turned = gg[at, :].astype(bf16).astype(f32) * conv.astype(f32)
        o_qg[:, at] = turned.T.astype(bf16)
        return 0

    lax.fori_loop(0, NCH, to_query_grad, 0, unroll=2)
    store_qg = pltpu.make_async_copy(o_qg, qg_hbm, store_sem.at[0])
    store_qg.start()

    received(seq_g, 3)
    convolve(seq_g, seq_z, gm_t, 4, True)
    far_r.wait_recv()
    p_right[low, :] = (sum_r[...] + from_l1[...].astype(f32)).astype(bf16)
    pass_r = chan_copy(p_right.at[low], from_l2.at[low], right, rs_send.at[4], rs_recv.at[4])
    pass_r.start()
    far_l.wait_recv()
    p_left[high, :] = (sum_l[...] + from_r1[...].astype(f32)).astype(bf16)
    pass_l = chan_copy(p_left.at[high], from_r2.at[high], left, rs_send.at[5], rs_recv.at[5])
    pass_l.start()

    own_z = pltpu.make_async_copy(seq_z.at[s], gm_t.at[s], store_sem.at[2])
    own_z.start()

    near_r.wait_recv()
    near_l.wait_recv()
    pass_r.wait_recv()
    pass_l.wait_recv()

    received(gm_t, 4)
    own_z.wait()
    sent(f_own, 0)
    for which, src in ((1, send_a), (2, seq_y), (3, send_g), (4, seq_z)):
        sent(src, which)
    for copy in (first_r, first_l, second_r, second_l, on_r, on_l):
        copy.wait_send()
    for copy in (far_r, far_l, near_r, near_l, pass_r, pass_l):
        copy.wait_send()
    for copy in (store_qg, store_own):
        copy.wait()


def finish_kernel(gm_t, k, v, qg_in, own, from_r, from_l, out, qg, kg, vg):
    width = out.shape[1]
    grad = gm_t[...].reshape(width, TOK).astype(f32).T
    kg[...] = (grad * v[...].astype(f32)).astype(bf16)
    vg[...] = (grad * k[...].astype(f32)).astype(bf16)
    qg[...] = qg_in[...]
    total = own[...].astype(f32) + from_r[...].astype(f32) + from_l[...].astype(f32)
    out[...] = total.astype(bf16)


def local(query, key, value, filters, weight, cotangent):
    stream = jax.ShapeDtypeStruct((TOK, WID), bf16)
    here = pl.BlockSpec(memory_space=pl.ANY)
    rows = pltpu.VMEM((TOK, WID), bf16)
    turned = pltpu.VMEM((SEQ, SUB, TOK), bf16)
    padded = pltpu.VMEM((SEQ + PAD, SUB, TOK), bf16)
    lines_at = pltpu.VMEM((SEQ, 2, CH), f32)
    half = pltpu.VMEM((HALF, WID), bf16)
    half_sum = pltpu.VMEM((HALF, WID), f32)
    dma = pltpu.SemaphoreType.DMA
    gm_t, query_grad, own, from_r, from_l = pl.pallas_call(
        kernel,
        out_shape=(jax.ShapeDtypeStruct((SEQ, SUB, TOK), bf16),) + (stream,) * 4,
        in_specs=[here] * 6,
        out_specs=(here,) * 5,
        scratch_shapes=[
            rows, rows, rows, rows,
            pltpu.VMEM((SEQ, TOK), bf16),
            lines_at,
            pltpu.VMEM((CHAN, WID, WID), bf16),
            lines_at,
            pltpu.VMEM((SEQ, TOK, TOK), bf16),
            turned, padded, turned, turned,
            pltpu.VMEM((WID, TOK), bf16),
            rows,
            pltpu.VMEM((PART * SUB, TOK), f32),
            turned, padded, turned,
            pltpu.VMEM((WID, TOK), f32),
            pltpu.VMEM((CHAN, TOK, WID), bf16),
            rows, rows, rows, rows,
            half, half,
            half_sum, half_sum,
            rows,
            dma((5,)), dma((CHAN,)), dma((3,)), dma((5,)), dma((5,)),
            dma((6,)), dma((6,)), dma((6,)), dma((6,)),
        ],
        compiler_params=pltpu.CompilerParams(
            collective_id=0, has_side_effects=True, vmem_limit_bytes=56 << 20
        ),
        cost_estimate=pl.CostEstimate(
            flops=18_000_000_000, bytes_accessed=12 << 20, transcendentals=0
        ),
    )(query, key, value, filters, weight, cotangent)
    width = 512
    cols = pl.BlockSpec((TOK, width), lambda j: (0, j))
    return pl.pallas_call(
        finish_kernel,
        out_shape=(stream,) * 4,
        grid=(WID // width,),
        in_specs=[pl.BlockSpec((width // SUB, SUB, TOK), lambda j: (j, 0, 0))] + [cols] * 6,
        out_specs=(cols,) * 4,
        cost_estimate=pl.CostEstimate(
            flops=4_000_000, bytes_accessed=6 << 20, transcendentals=0
        ),
    )(gm_t, key, value, query_grad, own, from_r, from_l)


def solution(mesh):
    split = P("seq", "chan")
    return jax.shard_map(
        local,
        mesh=mesh,
        in_specs=(split, split, split, P("chan", "seq"), P("chan", None), split),
        out_specs=(split,) * 4,
        check_vma=False,
    )
```

```python
import functools

import jax
import jax.numpy as jnp
from jax import lax
from jax.experimental import pallas as pl
from jax.experimental.pallas import tpu as pltpu
from jax.sharding import PartitionSpec as P

MESH = pl.DeviceIdType.MESH
f32, bf16 = jnp.float32, jnp.bfloat16
TOK = 256
WID = 1024
SEQ = 64
CHAN = 4
SUB = 16
PAD = 16
HALF = TOK // 2
CH = 128
NCH = WID // CH
PART = 16
PARTS = SEQ // PART
ROW = CH // SUB


def build_toeplitz(filt, toep):
    row = lax.broadcasted_iota(jnp.int32, (CH, CH), 0)
    col = lax.broadcasted_iota(jnp.int32, (CH, CH), 1)
    keep = col >= row

    def skew(k, half):
        line = filt[k, pl.ds(half, 1), :]
        return pltpu.roll(jnp.broadcast_to(line, (CH, CH)), 0, 1, stride=1, stride_axis=0)

    def step(k, carry):
        last_roll, last = carry
        first_roll = skew(k, 0)
        first = jnp.where(keep, first_roll, last_roll).astype(bf16)
        second_roll = skew(k, 1)
        second = jnp.where(keep, second_roll, first_roll).astype(bf16)
        toep[k, 0:CH, 0:CH] = first
        toep[k, 0:CH, CH:TOK] = second
        toep[k, CH:TOK, 0:CH] = last
        toep[k, CH:TOK, CH:TOK] = first
        return second_roll, second

    zero = jnp.zeros((CH, CH), f32)
    lax.fori_loop(0, SEQ, step, (zero, zero.astype(bf16)), unroll=4)


def conv_chunk(x, toep, acc, chunk, adjoint):
    unit = 8

    def step(m, _):
        k = m * unit
        first = PART * chunk + k if adjoint else PAD + PART * chunk - k
        sign = 1 if adjoint else -1
        left = jnp.concatenate(
            [x[pl.ds(first + sign * u, PART)].reshape(PART * SUB, TOK) for u in range(unit)], axis=1
        )
        if adjoint:
            right = jnp.concatenate([toep[k + u] for u in range(unit)], axis=1)
            part = lax.dot_general(
                left, right, (((1,), (1,)), ((), ())), preferred_element_type=f32
            )
        else:
            right = toep[pl.ds(k, unit)].reshape(unit * TOK, TOK)
            part = jnp.dot(left, right, preferred_element_type=f32)
        acc[...] += part
        return 0

    acc[...] = jnp.zeros_like(acc)
    steps = PART // unit
    lax.fori_loop(0, (PARTS - chunk) * steps if adjoint else (chunk + 1) * steps, step, 0)


def kernel(
    q_hbm, k_hbm, v_hbm, f_hbm, w_hbm, c_hbm,
    gm_t, qg_hbm, own_hbm, from_r2, from_l2,
    q, k, v, cot, f_raw, f_own, w, f_all, toep,
    send_a, seq_x, seq_y, conv_t, q_t, gated, acc,
    send_g, seq_g, seq_z, gg, cots,
    p_far, p_right, p_left, p_own, from_r1, from_l1, sum_r, sum_l, o_qg,
    load_sem, w_sem, store_sem, a2a_send, a2a_recv, ag_send, ag_recv, rs_send, rs_recv,
):
    s, c = lax.axis_index("seq"), lax.axis_index("chan")
    right, left, far = (lax.rem(c + d, CHAN) for d in (1, 3, 2))

    loads = [
        pltpu.make_async_copy(src, dst, load_sem.at[i])
        for i, (src, dst) in enumerate(
            ((k_hbm, k), (v_hbm, v), (f_hbm, f_raw), (c_hbm, cot), (q_hbm, q))
        )
    ]
    for copy in loads:
        copy.start()
    w_loads = [
        pltpu.make_async_copy(w_hbm.at[:, pl.ds(o * WID, WID)], w.at[o], w_sem.at[o])
        for o in range(CHAN)
    ]
    for copy in w_loads:
        copy.start()

    barrier = pltpu.get_barrier_semaphore()

    def greet(d, _):
        pl.semaphore_signal(barrier, inc=1, device_id=(lax.rem(s + d, SEQ), c), device_id_type=MESH)
        return 0

    lax.fori_loop(1, SEQ, greet, 0)
    for other in (right, left, far):
        pl.semaphore_signal(barrier, inc=1, device_id=(s, other), device_id_type=MESH)

    def send_block(src, dst, offset, which, to):
        @pl.when(to != s)
        def _():
            pltpu.make_async_remote_copy(
                src_ref=src.at[to],
                dst_ref=dst.at[offset + s],
                send_sem=a2a_send.at[which],
                recv_sem=a2a_recv.at[which],
                device_id=(to, c),
                device_id_type=MESH,
            ).start()

    def send_blocks(src, dst, offset, which, first, count):
        def step(d, _):
            send_block(src, dst, offset, which, first + lax.rem(lax.rem(s, count) + d, count))
            return 0

        lax.fori_loop(0, count, step, 0)

    def convolve(x, out, dst, which, adjoint):
        def step(i, _):
            chunk = lax.rem(s // PART + i, PARTS)
            conv_chunk(x, toep, acc, chunk, adjoint)
            at = pl.multiple_of(chunk * PART, PART)
            out[pl.ds(at, PART)] = acc[...].astype(bf16).reshape(PART, SUB, TOK)
            send_blocks(out, dst, 0, which, chunk * PART, PART)
            return 0

        lax.fori_loop(0, PARTS, step, 0)

    def received(dst, which):
        part = dst.at[pl.ds(0, SEQ - 1)]
        pltpu.make_async_copy(part, part, a2a_recv.at[which]).wait()

    def sent(src, which):
        part = src.at[pl.ds(0, SEQ - 1)]
        pltpu.make_async_copy(part, part, a2a_send.at[which]).wait()

    def chan_copy(src, dst, to, send, recv):
        return pltpu.make_async_remote_copy(
            src_ref=src,
            dst_ref=dst,
            send_sem=send,
            recv_sem=recv,
            device_id=(s, to),
            device_id_type=MESH,
        )

    pl.semaphore_wait(barrier, SEQ + CHAN - 2)

    low, high = pl.ds(0, HALF), pl.ds(HALF, HALF)
    first_r = chan_copy(c_hbm.at[low], cots.at[c, low], right, ag_send.at[0], ag_recv.at[0])
    first_l = chan_copy(c_hbm.at[high], cots.at[c, high], left, ag_send.at[1], ag_recv.at[1])
    second_r = chan_copy(c_hbm.at[high], cots.at[c, high], right, ag_send.at[2], ag_recv.at[2])
    second_l = chan_copy(c_hbm.at[low], cots.at[c, low], left, ag_send.at[3], ag_recv.at[3])
    on_r = chan_copy(cots.at[left, low], cots.at[left, low], right, ag_send.at[4], ag_recv.at[4])
    on_l = chan_copy(cots.at[right, high], cots.at[right, high], left, ag_send.at[5], ag_recv.at[5])

    loads[2].wait()
    lines = f_raw[...].astype(f32)
    f_own[:, 0, :] = lines[:, 0:CH]
    f_own[:, 1, :] = lines[:, CH:TOK]
    send_blocks(f_own, f_all, 0, 0, 0, SEQ)
    loads[0].wait()
    loads[1].wait()

    def mix(i, _):
        j = lax.rem(s // ROW + i, NCH)
        at = pl.ds(pl.multiple_of(j * CH, CH), CH)
        mixed = (k[:, at].astype(f32) * v[:, at].astype(f32)).astype(bf16)
        turned = mixed.astype(f32).T.astype(bf16)
        send_a[pl.ds(j * ROW, ROW)] = turned.reshape(ROW, SUB, TOK)
        send_blocks(send_a, seq_x, PAD, 1, j * ROW, ROW)
        return 0

    lax.fori_loop(0, NCH, mix, 0, unroll=2)
    first_r.start()
    first_l.start()
    second_r.start()
    second_l.start()
    f_all[s] = f_own[s]
    seq_x[PAD + s] = send_a[s]
    seq_x[0:PAD] = jnp.zeros((PAD, SUB, TOK), bf16)
    seq_g[SEQ : SEQ + PAD] = jnp.zeros((PAD, SUB, TOK), bf16)

    loads[4].wait()

    def turn_q(j, _):
        at = pl.ds(pl.multiple_of(j * CH, CH), CH)
        q_t[pl.ds(pl.multiple_of(j * CH, CH), CH), :] = q[:, at].astype(f32).T.astype(bf16)
        return 0

    lax.fori_loop(0, NCH, turn_q, 0, unroll=2)

    received(f_all, 0)
    build_toeplitz(f_all, toep)

    first_r.wait_recv()
    on_r.start()
    first_l.wait_recv()
    on_l.start()

    received(seq_x, 1)
    convolve(seq_x, seq_y, conv_t, 2, False)
    conv_t[s] = seq_y[s]

    loads[3].wait()
    for copy in w_loads:
        copy.wait()

    def grad_part(owner, block, start):
        def step(j, _):
            rows = pl.ds(pl.multiple_of(j * TOK, TOK), TOK)
            part = lax.dot_general(
                w[owner, rows, :], block[...], (((1,), (1,)), ((), ())), preferred_element_type=f32
            )
            if start:
                gg[rows, :] = part
            else:
                gg[rows, :] += part
            return 0

        lax.fori_loop(0, WID // TOK, step, 0, unroll=2)

    grad_part(c, cot, True)
    second_r.wait_recv()
    grad_part(left, cots.at[left], False)
    second_l.wait_recv()
    grad_part(right, cots.at[right], False)
    on_r.wait_recv()
    on_l.wait_recv()
    grad_part(far, cots.at[far], False)

    def to_grad_conv(i, _):
        j = lax.rem(s // ROW + i, NCH)
        at = pl.ds(pl.multiple_of(j * CH, CH), CH)
        rounded = gg[at, :].astype(bf16).astype(f32)
        grad_conv = (rounded * q_t[at, :].astype(f32)).astype(bf16)
        send_g[pl.ds(j * ROW, ROW)] = grad_conv.reshape(ROW, SUB, TOK)
        send_blocks(send_g, seq_g, 0, 3, j * ROW, ROW)
        return 0

    lax.fori_loop(0, NCH, to_grad_conv, 0, unroll=2)
    seq_g[s] = send_g[s]


    received(conv_t, 2)

    def gate(j, _):
        at = pl.ds(pl.multiple_of(j * CH, CH), CH)
        conv = conv_t[pl.ds(j * ROW, ROW)].reshape(CH, TOK)
        turned = (q_t[at, :].astype(f32) * conv.astype(f32)).astype(bf16)
        gated[:, at] = turned.astype(f32).T.astype(bf16)
        return 0

    lax.fori_loop(0, NCH, gate, 0, unroll=2)

    def output_part(owner, dst, keep=None, keep_rows=None):
        def step(j, _):
            at = pl.ds(pl.multiple_of(j * TOK, TOK), TOK)
            part = jnp.dot(gated[...], w[owner, :, at], preferred_element_type=f32)
            dst[:, at] = part.astype(dst.dtype)
            if keep is not None:
                keep[:, at] = part[keep_rows]
            return 0

        lax.fori_loop(0, WID // TOK, step, 0, unroll=2)

    far_r = chan_copy(p_far.at[low], from_l1, right, rs_send.at[0], rs_recv.at[0])
    far_l = chan_copy(p_far.at[high], from_r1, left, rs_send.at[1], rs_recv.at[1])
    near_r = chan_copy(p_right.at[high], from_l2.at[high], right, rs_send.at[2], rs_recv.at[2])
    near_l = chan_copy(p_left.at[low], from_r2.at[low], left, rs_send.at[3], rs_recv.at[3])

    output_part(far, p_far)
    far_r.start()
    far_l.start()
    output_part(right, p_right, sum_r, slice(0, HALF))
    near_r.start()
    output_part(left, p_left, sum_l, slice(HALF, TOK))
    near_l.start()
    output_part(c, p_own)
    store_own = pltpu.make_async_copy(p_own, own_hbm, store_sem.at[1])
    store_own.start()

    def to_query_grad(j, _):
        at = pl.ds(pl.multiple_of(j * CH, CH), CH)
        conv = conv_t[pl.ds(j * ROW, ROW)].reshape(CH, TOK)
        turned = gg[at, :].astype(bf16).astype(f32) * conv.astype(f32)
        o_qg[:, at] = turned.T.astype(bf16)
        return 0

    lax.fori_loop(0, NCH, to_query_grad, 0, unroll=2)
    store_qg = pltpu.make_async_copy(o_qg, qg_hbm, store_sem.at[0])
    store_qg.start()

    received(seq_g, 3)
    convolve(seq_g, seq_z, gm_t, 4, True)
    far_r.wait_recv()
    p_right[low, :] = (sum_r[...] + from_l1[...].astype(f32)).astype(bf16)
    pass_r = chan_copy(p_right.at[low], from_l2.at[low], right, rs_send.at[4], rs_recv.at[4])
    pass_r.start()
    far_l.wait_recv()
    p_left[high, :] = (sum_l[...] + from_r1[...].astype(f32)).astype(bf16)
    pass_l = chan_copy(p_left.at[high], from_r2.at[high], left, rs_send.at[5], rs_recv.at[5])
    pass_l.start()

    own_z = pltpu.make_async_copy(seq_z.at[s], gm_t.at[s], store_sem.at[2])
    own_z.start()

    near_r.wait_recv()
    near_l.wait_recv()
    pass_r.wait_recv()
    pass_l.wait_recv()

    received(gm_t, 4)
    own_z.wait()
    sent(f_own, 0)
    for which, src in ((1, send_a), (2, seq_y), (3, send_g), (4, seq_z)):
        sent(src, which)
    for copy in (first_r, first_l, second_r, second_l, on_r, on_l):
        copy.wait_send()
    for copy in (far_r, far_l, near_r, near_l, pass_r, pass_l):
        copy.wait_send()
    for copy in (store_qg, store_own):
        copy.wait()


def finish_kernel(gm_t, k, v, qg_in, own, from_r, from_l, out, qg, kg, vg):
    width = out.shape[1]
    grad = gm_t[...].reshape(width, TOK).astype(f32).T
    kg[...] = (grad * v[...].astype(f32)).astype(bf16)
    vg[...] = (grad * k[...].astype(f32)).astype(bf16)
    qg[...] = qg_in[...]
    total = own[...].astype(f32) + from_r[...].astype(f32) + from_l[...].astype(f32)
    out[...] = total.astype(bf16)


def local(query, key, value, filters, weight, cotangent):
    stream = jax.ShapeDtypeStruct((TOK, WID), bf16)
    here = pl.BlockSpec(memory_space=pl.ANY)
    rows = pltpu.VMEM((TOK, WID), bf16)
    turned = pltpu.VMEM((SEQ, SUB, TOK), bf16)
    padded = pltpu.VMEM((SEQ + PAD, SUB, TOK), bf16)
    lines_at = pltpu.VMEM((SEQ, 2, CH), f32)
    half = pltpu.VMEM((HALF, WID), bf16)
    half_sum = pltpu.VMEM((HALF, WID), f32)
    dma = pltpu.SemaphoreType.DMA
    gm_t, query_grad, own, from_r, from_l = pl.pallas_call(
        kernel,
        out_shape=(jax.ShapeDtypeStruct((SEQ, SUB, TOK), bf16),) + (stream,) * 4,
        in_specs=[here] * 6,
        out_specs=(here,) * 5,
        scratch_shapes=[
            rows, rows, rows, rows,
            pltpu.VMEM((SEQ, TOK), bf16),
            lines_at,
            pltpu.VMEM((CHAN, WID, WID), bf16),
            lines_at,
            pltpu.VMEM((SEQ, TOK, TOK), bf16),
            turned, padded, turned, turned,
            pltpu.VMEM((WID, TOK), bf16),
            rows,
            pltpu.VMEM((PART * SUB, TOK), f32),
            turned, padded, turned,
            pltpu.VMEM((WID, TOK), f32),
            pltpu.VMEM((CHAN, TOK, WID), bf16),
            rows, rows, rows, rows,
            half, half,
            half_sum, half_sum,
            rows,
            dma((5,)), dma((CHAN,)), dma((3,)), dma((5,)), dma((5,)),
            dma((6,)), dma((6,)), dma((6,)), dma((6,)),
        ],
        compiler_params=pltpu.CompilerParams(
            collective_id=0, has_side_effects=True, vmem_limit_bytes=56 << 20
        ),
        cost_estimate=pl.CostEstimate(
            flops=18_000_000_000, bytes_accessed=12 << 20, transcendentals=0
        ),
    )(query, key, value, filters, weight, cotangent)
    width = 512
    cols = pl.BlockSpec((TOK, width), lambda j: (0, j))
    return pl.pallas_call(
        finish_kernel,
        out_shape=(stream,) * 4,
        grid=(WID // width,),
        in_specs=[pl.BlockSpec((width // SUB, SUB, TOK), lambda j: (j, 0, 0))] + [cols] * 6,
        out_specs=(cols,) * 4,
        cost_estimate=pl.CostEstimate(
            flops=4_000_000, bytes_accessed=6 << 20, transcendentals=0
        ),
    )(gm_t, key, value, query_grad, own, from_r, from_l)


def solution(mesh):
    split = P("seq", "chan")
    return jax.shard_map(
        local,
        mesh=mesh,
        in_specs=(split, split, split, P("chan", "seq"), P("chan", None), split),
        out_specs=(split,) * 4,
        check_vma=False,
    )
```
